32 devices in a mesh: img: 4 (over y, core), fsdp: 8 (over z, x).
Axes of the slice: x: 2, y: 2, z: 4, core: 2. Of those that a mesh axis runs over, the one named last changes fastest.
Arguments:
- text_states: bfloat16 [2048, 8192], P('img', 'fsdp'), may hold values from -100 to 100, as said below
- text_gain: float32 [8192], P('fsdp'), may hold values from 0.1 to 1.9
- gate_scale: float32 [8192], P('fsdp'), may hold values from 0.3 to 1.5
- live_counts: int32 [4], P('img'), may hold values from 1 to 512, 1536 in all
- token_slot: int32 [4, 512], P('img'), may hold values from 0 to 7, never falling along the last dimension, each value on 1 to 256 neighbouring positions
- wanted_images: int32 [4, 8], replicated, may hold values from 0 to 15, as said below
- patches: bfloat16 [16, 256, 1280], P('img', None, 'fsdp'), may hold values from -100 to 100, as said below
- latent_init: bfloat16 [64, 1280], replicated, may hold values from -100 to 100, as said below
- context_gain: float32 [1280], replicated, may hold values from 0.1 to 1.9
- latent_gain: float32 [1280], replicated, may hold values from 0.1 to 1.9
- res_query: bfloat16 [1280, 1536], P(None, 'fsdp'), may hold values from -0.15625 to 0.15625
- res_key: bfloat16 [1280, 1536], P(None, 'fsdp'), may hold values from -0.15625 to 0.15625
- res_value: bfloat16 [1280, 1536], P(None, 'fsdp'), may hold values from -0.15625 to 0.15625
- res_out: bfloat16 [1536, 1280], P('fsdp'), may hold values from -0.21875 to 0.21875
- final_gain: float32 [1280], P('fsdp'), may hold values from 0.1 to 1.9
- cross_query: bfloat16 [8192, 8192], P('fsdp'), may hold values from -0.09375 to 0.09375
- cross_key: bfloat16 [1280, 8192], P('fsdp'), may hold values from -0.25 to 0.25
- cross_value: bfloat16 [1280, 8192], P('fsdp'), may hold values from -0.25 to 0.25
- cross_out: bfloat16 [8192, 8192], P('fsdp'), may hold values from -0.09375 to 0.09375
Outputs:
- layer_output: float32 [2048, 8192], P('img', 'fsdp')
The draws below stay inside these ranges and needn't reach their ends.
Inputs may be any that keep to these rules, and one draw needn't show every extreme that they name: `wanted_images`: image i is held by owner i // 4 along img. A row lists 8 distinct images; every owner that appears in a row has exactly 2 of its images there. `token_slot`: along a shard's tokens the slot never falls, and every slot of the shard is used. Tokens of shard s at positions live_counts[s] and beyond are padding. `text_states`: real values. `patches`: real values. `latent_init`: real values.
All inputs are finite; a program needn't handle non-finite values.
Results may differ from the reference program's by a relative error of at most 0.0075.
Values may be sent and summed in bfloat16 or wider, within the bound.
A program may use at most 128 MiB of HBM per device.

```python
import math
import jax
import jax.numpy as jnp
import numpy as np
from jax import lax

D = 8192
QH = 64
HEAD = 128
VIS = 1280
RH = 16
RHD = 96
R = 64
P_SIZE = 256
CAP = 8
PAIR = 2
IMG_DEV = 4
TOK_DEV = 512
HD = 8192
RINNER = 1536
SHARDS = 4
IMAGES = 16
TEXT = 2048
N_FSDP = 8


def scaled_field(field_key, row_total, col_total):
    first_key, second_key = jax.random.split(field_key, 2)
    col_pos = jnp.arange(col_total, dtype=jnp.float32) / col_total
    row_pos = jax.random.uniform(second_key, (row_total, 1), dtype=jnp.float32)
    noise_base = jnp.clip(jax.random.normal(first_key, (row_total, col_total), dtype=jnp.float32), -6.0, 6.0)
    field_scale = 10.0 ** (col_pos + row_pos - 1.0)
    return noise_base * field_scale


def draw_text_states(key, part):
    return scaled_field(jax.random.fold_in(key, 11), TEXT, D).astype(jnp.bfloat16)


def draw_patches(key, part):
    field = scaled_field(jax.random.fold_in(key, 12), IMAGES * P_SIZE, VIS)
    return field.reshape(IMAGES, P_SIZE, VIS).astype(jnp.bfloat16)


def draw_latent_init(key, part):
    return scaled_field(jax.random.fold_in(key, 13), R, VIS).astype(jnp.bfloat16)


def draw_wanted_images(key, part):
    base_key = jax.random.fold_in(key, 14)

    def one_shard(shard_key):
        owner_key, pick_key, order_key = jax.random.split(shard_key, 3)
        owners = jax.random.permutation(owner_key, SHARDS)[:CAP // PAIR]
        pick_keys = jax.random.split(pick_key, CAP // PAIR)
        picks = jax.vmap(lambda inner_key: jax.random.permutation(inner_key, IMG_DEV)[:PAIR])(pick_keys)
        listed = (owners[:, None] * IMG_DEV + picks).reshape(CAP)
        return jax.random.permutation(order_key, listed)
    return jax.vmap(one_shard)(jax.random.split(base_key, SHARDS)).astype(jnp.int32)


def with_spikes(entries, own_key, source, target, parts, factor):
    def block_of(dim):
        return (jnp.arange(entries.shape[dim]) // (entries.shape[dim] // parts)).reshape((-1,) + (1,) * (entries.ndim - 1 - dim))

    first = jax.random.permutation(own_key, parts)[block_of(target)]
    far = (block_of(target) + parts // 2) % parts
    return jnp.where((block_of(source) == first) | (block_of(source) == far), factor * entries, entries)


def block_scale(stream_key, extent, cuts, low, largest):
    loudness, own = 1.0, jax.random.fold_in(stream_key, 6)
    for dim, parts in cuts:
        steps = jnp.exp(jax.random.uniform(jax.random.fold_in(own, dim), (parts,), jnp.float32, low / len(cuts), largest / len(cuts)))
        loudness = loudness * jnp.repeat(steps, extent[dim] // parts).reshape([-1 if axis == dim else 1 for axis in range(len(extent))])
    return loudness


def length_profile(number_of, total, limit, lean):
    loads = [(1 << 20) // math.isqrt(grade ** lean) + 1 for grade in range(2, number_of + 1)]
    spare, counts = total - limit - (number_of - 1), [1] * (number_of - 1)
    while spare > 0:
        candidates = [i for i in range(number_of - 1) if counts[i] < limit]
        mass, remaining = sum([loads[i] for i in candidates]), spare
        for i in candidates:
            more = min(limit - counts[i], max(1, remaining * loads[i] // mass), spare)
            counts[i] = counts[i] + more
            spare = spare - more
    return np.array([limit] + counts)


def ragged(rng, amount, total, reach, skew):
    if amount == 2:
        one = jax.random.randint(rng, (), max(1, total - reach), min(reach, total - 1) + 1)
        return jnp.stack([one, total - one])
    lengths = jnp.asarray(length_profile(amount, total, reach, skew), jnp.int32)
    couples = (amount - 1) // 2
    source_of, taker = lengths[1:1 + 2 * couples:2], lengths[2:2 + 2 * couples:2]
    slack = jnp.minimum(source_of - 1, reach - taker)
    moved = jax.random.randint(jax.random.fold_in(rng, 1), (couples,), 0, 1 << 20) % (slack + 1)
    lengths = lengths.at[1:1 + 2 * couples:2].set(source_of - moved).at[2:2 + 2 * couples:2].set(taker + moved)
    return lengths[jax.random.permutation(jax.random.fold_in(rng, 2), amount)]


def scatter_about(own_key, shape, scale, limit, cuts=(), kind=jnp.bfloat16):
    drawn = jax.random.normal(own_key, shape, jnp.float32) * scale
    if len(cuts) > 0:
        drawn = block_scale(own_key, shape, cuts, -0.22, 0.18) * drawn
    return jnp.clip(drawn, min=-limit, max=limit).astype(kind)


def noise_with(stream_key, extent, scale, limit, shards, heavy, kind=jnp.bfloat16):
    values = scale * jax.random.normal(stream_key, extent, jnp.float32)
    if shards:
        values = values * block_scale(stream_key, extent, shards, -0.22, 0.18)
    return jnp.clip(with_spikes(values, jax.random.fold_in(stream_key, 3), *heavy), -limit, limit).astype(kind)


def setup_inputs(seed: int = 0) -> dict:
    streams_of = jax.random.split(jax.random.key(seed), 20)
    return {
        "text_states": draw_text_states(jax.random.fold_in(streams_of[19], 71), 0),
        "text_gain": jnp.clip(1.0 + 0.18 * jax.random.normal(streams_of[1], (D,), jnp.float32), 0.1, 1.9),
        "gate_scale": jnp.clip(0.3 + 1.2 * jax.random.uniform(streams_of[2], (D,), jnp.float32) ** block_scale(streams_of[2], (D,), ((0, 8),), -0.2, 0.2), 0.3, 1.5),
        "live_counts": ragged(streams_of[3], SHARDS, SHARDS * TOK_DEV * 3 // 4, TOK_DEV, 1).astype(jnp.int32),
        "token_slot": jax.vmap(lambda own: jnp.searchsorted(jnp.cumsum(ragged(own, CAP, TOK_DEV, TOK_DEV // 2, 1)), jnp.arange(TOK_DEV), side="right"))(jax.random.split(streams_of[4], SHARDS)).reshape((SHARDS, TOK_DEV)).astype(jnp.int32),
        "wanted_images": draw_wanted_images(jax.random.fold_in(streams_of[19], 71), 0),
        "patches": draw_patches(jax.random.fold_in(streams_of[19], 71), 0),
        "latent_init": draw_latent_init(jax.random.fold_in(streams_of[19], 71), 0),
        "context_gain": jnp.clip(1.0 + 0.18 * jax.random.normal(streams_of[8], (VIS,), jnp.float32), 0.1, 1.9),
        "latent_gain": jnp.clip(1.0 + 0.18 * jax.random.normal(streams_of[9], (VIS,), jnp.float32), 0.1, 1.9),
        "res_query": scatter_about(streams_of[10], (VIS, RINNER), VIS ** -0.5, 0.15625, ((1, 8),)),
        "res_key": scatter_about(streams_of[11], (VIS, RINNER), VIS ** -0.5, 0.15625, ((1, 8),)),
        "res_value": scatter_about(streams_of[12], (VIS, RINNER), VIS ** -0.5, 0.15625, ((1, 8),)),
        "res_out": noise_with(streams_of[13], (RINNER, VIS), RINNER ** -0.5, 0.21875, ((0, 8),), (0, 1, 8, 2.0)),
        "final_gain": jnp.clip(1.0 + 0.18 * jax.random.normal(streams_of[14], (VIS,), jnp.float32), 0.1, 1.9),
        "cross_query": noise_with(streams_of[15], (D, HD), D ** -0.5, 0.09375, ((0, 8),), (0, 1, 8, 2.0)),
        "cross_key": noise_with(streams_of[16], (VIS, HD), VIS ** -0.5, 0.25, ((0, 8),), (0, 1, 8, 2.0)),
        "cross_value": noise_with(streams_of[17], (VIS, HD), VIS ** -0.5, 0.25, ((0, 8),), (0, 1, 8, 2.0)),
        "cross_out": noise_with(streams_of[18], (HD, D), HD ** -0.5, 0.09375, ((0, 8),), (0, 1, 8, 2.0)),
    }


eps_norm = 1e-05
eps_rms = 1e-06

def layer_norm(values, gain_vec):
    values = values.astype(jnp.float32)
    row_mean = lax.optimization_barrier(jnp.mean(values, -1, keepdims=True))
    spread = lax.optimization_barrier(jnp.mean(values * values, -1, keepdims=True)) - row_mean * row_mean
    return (values - row_mean) * lax.rsqrt(spread + eps_norm) * gain_vec

def block_sum(left, right, blocks):
    block_width = left.shape[1] // blocks
    running = jnp.zeros((left.shape[0], right.shape[1]), jnp.float32)
    for block in range(blocks):
        lower = block * block_width
        product = jnp.dot(left[:, lower:lower + block_width], right[lower:lower + block_width], preferred_element_type=jnp.float32)
        running = running + lax.optimization_barrier(product.astype(jnp.bfloat16)).astype(jnp.float32)
    return running

def reference(text_states, text_gain, gate_scale, live_counts, token_slot, wanted_images, patches, latent_init, context_gain, latent_gain, res_query, res_key, res_value, res_out, final_gain, cross_query, cross_key, cross_value, cross_out):
    context = layer_norm(patches, context_gain).astype(jnp.bfloat16)
    latent_normed = layer_norm(latent_init, latent_gain).astype(jnp.bfloat16)
    res_q_rows = jnp.dot(latent_normed, res_query, preferred_element_type=jnp.float32).astype(jnp.bfloat16)
    query_split = res_q_rows.reshape(R, RH, RHD).astype(jnp.float32)
    res_scale = RHD ** (-0.5)

    def resample(image_rows):
        joined = jnp.concatenate([image_rows, latent_normed], 0)
        key_rows = jnp.dot(joined, res_key, preferred_element_type=jnp.float32).astype(jnp.bfloat16)
        value_rows = jnp.dot(joined, res_value, preferred_element_type=jnp.float32).astype(jnp.bfloat16)
        key_rows = key_rows.reshape(P_SIZE + R, RH, RHD).astype(jnp.float32)
        value_rows = value_rows.reshape(P_SIZE + R, RH, RHD).astype(jnp.float32)
        scores = jnp.einsum('rhe,khe->hrk', query_split, key_rows) * res_scale
        weights = jnp.exp(scores)
        weights = (weights / lax.optimization_barrier(jnp.sum(weights, -1, keepdims=True))).astype(jnp.bfloat16)
        mixed = jnp.einsum('hrk,khe->rhe', weights.astype(jnp.float32), value_rows)
        return mixed.astype(jnp.bfloat16).reshape(R, RINNER)
    mixed_all = lax.map(resample, context)
    mixed_proj = jnp.dot(mixed_all.reshape(IMAGES * R, RINNER), res_out, preferred_element_type=jnp.float32)
    latents = latent_init.astype(jnp.float32)[None] + mixed_proj.reshape(IMAGES, R, VIS)
    resampled = layer_norm(latents, final_gain).astype(jnp.bfloat16)
    text_f = text_states.astype(jnp.float32)
    normed = (text_f * lax.rsqrt(lax.optimization_barrier(jnp.mean(text_f * text_f, -1, keepdims=True)) + eps_rms) * text_gain).astype(jnp.bfloat16)
    query_all = block_sum(normed, cross_query, N_FSDP).astype(jnp.bfloat16)
    flat_latents = resampled.reshape(IMAGES * R, VIS)
    key_all = block_sum(flat_latents, cross_key, N_FSDP).astype(jnp.bfloat16).reshape(IMAGES, R, QH, HEAD)
    value_all = block_sum(flat_latents, cross_value, N_FSDP).astype(jnp.bfloat16).reshape(IMAGES, R, QH, HEAD)
    cross_scale = HEAD ** (-0.5)

    def attend(shard_inputs):
        shard_query, shard_slots, shard_images = shard_inputs
        slot_keys = key_all[shard_images].astype(jnp.float32)
        slot_values = value_all[shard_images].astype(jnp.float32)
        query_heads = shard_query.reshape(TOK_DEV, QH, HEAD).astype(jnp.float32)
        scores = jnp.einsum('the,crhe->htcr', query_heads, slot_keys) * cross_scale
        slot_hot = (shard_slots[:, None] == jnp.arange(CAP, dtype=jnp.int32)[None, :]).astype(jnp.float32)
        weights = jnp.exp(scores) * slot_hot[None, :, :, None]
        weights = (weights / lax.optimization_barrier(jnp.sum(weights, axis=(2, 3), keepdims=True))).astype(jnp.bfloat16)
        mixed = jnp.einsum('htcr,crhe->the', weights.astype(jnp.float32), slot_values)
        return mixed.astype(jnp.bfloat16).reshape(TOK_DEV, HD)
    attended = lax.map(attend, (query_all.reshape(SHARDS, TOK_DEV, HD), token_slot, wanted_images)).reshape(TEXT, HD)
    projected = block_sum(attended, cross_out, N_FSDP)
    positions = jnp.arange(TOK_DEV, dtype=jnp.int32)
    live_mask = (positions[None, :] < live_counts[:, None]).astype(jnp.float32).reshape(TEXT, 1)
    return text_f + jnp.tanh(gate_scale) * projected * live_mask
```

```python
import functools

import jax
import jax.numpy as jnp
from jax import lax
from jax.experimental import pallas as pl
from jax.experimental.pallas import tpu as pltpu
from jax.sharding import PartitionSpec as P

D = 8192
HEAD = 128
RHD = 96
PAIR = 2


eps_norm = 1e-05
eps_rms = 1e-06


def layer_norm(values, gain_vec):
    values = values.astype(jnp.float32)
    row_mean = jnp.mean(values, -1, keepdims=True)
    spread = jnp.mean(values * values, -1, keepdims=True) - row_mean * row_mean
    return (values - row_mean) * lax.rsqrt(spread + eps_norm) * gain_vec


def route_tables(wanted_images, per_owner, pair_slots):
    owners = wanted_images // per_owner
    slot_total = wanted_images.shape[1]
    positions = jnp.arange(slot_total, dtype=jnp.int32)
    before = (owners[:, :, None] == owners[:, None, :]) & (
        positions[None, None, :] < positions[None, :, None]
    )
    slot_rank = jnp.sum(before.astype(jnp.int32), axis=2)
    rank_hot = (
        slot_rank[:, :, None] == jnp.arange(pair_slots, dtype=jnp.int32)[None, None, :]
    ).astype(jnp.float32)
    return (owners, rank_hot)


def pack_rows(row_data, wanted_images, my_shard, per_owner, pair_slots):
    owners, rank_hot = route_tables(wanted_images, per_owner, pair_slots)
    is_mine = (owners == my_shard).astype(jnp.float32)
    local_hot = (
        (wanted_images % per_owner)[:, :, None]
        == jnp.arange(per_owner, dtype=jnp.int32)[None, None, :]
    ).astype(jnp.float32)
    picker = jnp.einsum("scp,sci->spi", rank_hot * is_mine[:, :, None], local_hot).astype(
        jnp.bfloat16
    )
    return jnp.einsum("spi,if->spf", picker, row_data, preferred_element_type=jnp.float32).astype(
        jnp.bfloat16
    )


def unpack_rows(received, wanted_images, my_shard, per_owner, pair_slots):
    owners, rank_hot = route_tables(wanted_images, per_owner, pair_slots)
    owner_row = lax.dynamic_slice_in_dim(owners, my_shard, 1, 0)[0]
    rank_row = lax.dynamic_slice_in_dim(rank_hot, my_shard, 1, 0)[0]
    source_hot = (
        owner_row[:, None] == jnp.arange(received.shape[0], dtype=jnp.int32)[None, :]
    ).astype(jnp.float32)
    taker = (source_hot[:, :, None] * rank_row[:, None, :]).astype(jnp.bfloat16)
    return jnp.einsum("cop,opf->cf", taker, received, preferred_element_type=jnp.float32).astype(
        jnp.bfloat16
    )


MESH = pl.DeviceIdType.MESH
LINE = 4
HALVES = 2
TILE = 256


def remote(src, dst, send, recv, target):
    return pltpu.make_async_remote_copy(
        src_ref=src,
        dst_ref=dst,
        send_sem=send,
        recv_sem=recv,
        device_id={"fsdp": target},
        device_id_type=MESH,
    )


def product_scatter_kernel(
    rows_ref, weight_ref, out_ref,
    weight, own, x_out, x_in, z_out, z_in,
    w_sem, x_send, x_recv, z_send, z_recv,
):
    me = lax.axis_index("fsdp")
    line, side = me // 2, me % 2
    across = line * 2 + (1 - side)
    is_end = (line == 0) | (line == LINE - 1)
    is_mid = jnp.logical_not(is_end)
    low = line < 2
    near_line = jnp.where(line % 2 == 0, line + 1, line - 1)
    near = near_line * 2 + side
    other_mid = (LINE - 1 - line) * 2 + side
    places = (
        jnp.where(low, 3, 0),
        jnp.where(low, 2, 1),
        near_line,
        line,
    )
    width = weight.shape[2]
    half = width // HALVES

    def fetch(slot):
        step, part = slot % LINE, slot // LINE
        block = places[step] * 2 + (side if part else 1 - side)
        return pltpu.make_async_copy(
            weight_ref.at[:, pl.ds(pl.multiple_of(block * width, width), width)],
            weight.at[slot],
            w_sem.at[slot],
        )

    for slot in range(2 * LINE):
        fetch(slot).start()

    barrier = pltpu.get_barrier_semaphore()
    for target in (across, near):
        pl.semaphore_signal(barrier, inc=1, device_id={"fsdp": target}, device_id_type=MESH)

    @pl.when(is_mid)
    def _():
        pl.semaphore_signal(barrier, inc=1, device_id={"fsdp": other_mid}, device_id_type=MESH)
        pl.semaphore_wait(barrier, 3)

    @pl.when(is_end)
    def _():
        pl.semaphore_wait(barrier, 2)

    def multiply(slot, into, step):
        for h in range(HALVES):

            def tile(c, carry, h=h):
                lower = pl.multiple_of(c * TILE, TILE)
                into[step, h, :, pl.ds(lower, TILE)] = jnp.dot(
                    rows_ref[...],
                    weight[slot, :, pl.ds(pl.multiple_of(h * half + lower, TILE), TILE)],
                    preferred_element_type=jnp.float32,
                ).astype(into.dtype)
                return carry

            lax.fori_loop(0, half // TILE, tile, 0)

    def x_copy(step, h):
        return remote(
            x_out.at[step, h], x_in.at[step, h], x_send.at[step, h], x_recv.at[step, h], across
        )

    def z_copy(step, h):
        if step < 2:
            slot, target = jnp.where(is_end, step, 3 + step), jnp.where(is_end, near, other_mid)
        else:
            slot, target = jnp.where(is_end, 2, 0), near
        return remote(
            z_out.at[step, h], z_in.at[slot, h], z_send.at[step, h], z_recv.at[slot, h], target
        )

    def z_arrived(slot, h):
        remote(
            z_out.at[0, h], z_in.at[slot, h], z_send.at[0, h], z_recv.at[slot, h], near
        ).wait_recv()

    for step in range(LINE):
        fetch(step).wait()
        multiply(step, x_out, step)
        for h in range(HALVES):
            x_copy(step, h).start()
    for step in range(LINE):
        fetch(LINE + step).wait()
        multiply(LINE + step, own, step)

    for step in range(LINE):
        for h in range(HALVES):
            x_copy(step, h).wait_recv()
            if step < LINE - 1:
                arriving = step if step < 2 else 3

                @pl.when(is_end)
                def _(step=step, h=h):
                    z_out[step, h] = (
                        own[step, h].astype(jnp.float32) + x_in[step, h].astype(jnp.float32)
                    ).astype(z_out.dtype)

                @pl.when(is_mid)
                def _(step=step, h=h, arriving=arriving):
                    z_arrived(arriving, h)
                    z_out[step, h] = (
                        own[step, h].astype(jnp.float32)
                        + x_in[step, h].astype(jnp.float32)
                        + z_in[arriving, h].astype(jnp.float32)
                    ).astype(z_out.dtype)

                z_copy(step, h).start()
            else:

                @pl.when(is_end)
                def _(step=step, h=h):
                    z_arrived(0, h)
                    out_ref[:, h * half : (h + 1) * half] = (
                        own[step, h].astype(jnp.float32)
                        + x_in[step, h].astype(jnp.float32)
                        + z_in[0, h].astype(jnp.float32)
                    )

                @pl.when(is_mid)
                def _(step=step, h=h):
                    z_arrived(2, h)
                    z_arrived(4, h)
                    out_ref[:, h * half : (h + 1) * half] = (
                        own[step, h].astype(jnp.float32)
                        + x_in[step, h].astype(jnp.float32)
                        + z_in[2, h].astype(jnp.float32)
                        + z_in[4, h].astype(jnp.float32)
                    )

    for step in range(LINE):
        for h in range(HALVES):
            x_copy(step, h).wait_send()
            if step < LINE - 1:
                z_copy(step, h).wait_send()


def product_scatter(rows, weight, collective_id):
    size = lax.axis_size("fsdp")
    if size != 2 * LINE:
        part = jnp.dot(rows, weight, preferred_element_type=jnp.float32).astype(jnp.bfloat16)
        return lax.psum_scatter(part, "fsdp", scatter_dimension=1, tiled=True).astype(jnp.float32)
    count, depth = rows.shape
    width = weight.shape[1] // size
    unit = (HALVES, count, width // HALVES)
    return pl.pallas_call(
        product_scatter_kernel,
        out_shape=jax.ShapeDtypeStruct((count, width), jnp.float32),
        in_specs=[
            pl.BlockSpec(memory_space=pltpu.VMEM),
            pl.BlockSpec(memory_space=pl.ANY),
        ],
        out_specs=pl.BlockSpec(memory_space=pltpu.VMEM),
        scratch_shapes=[
            pltpu.VMEM((2 * LINE, depth, width), jnp.bfloat16),
            pltpu.VMEM((LINE,) + unit, jnp.bfloat16),
            pltpu.VMEM((LINE,) + unit, jnp.bfloat16),
            pltpu.VMEM((LINE,) + unit, jnp.bfloat16),
            pltpu.VMEM((LINE - 1,) + unit, jnp.bfloat16),
            pltpu.VMEM((LINE + 1,) + unit, jnp.bfloat16),
            pltpu.SemaphoreType.DMA((2 * LINE,)),
            pltpu.SemaphoreType.DMA((LINE, HALVES)),
            pltpu.SemaphoreType.DMA((LINE, HALVES)),
            pltpu.SemaphoreType.DMA((LINE - 1, HALVES)),
            pltpu.SemaphoreType.DMA((LINE + 1, HALVES)),
        ],
        compiler_params=pltpu.CompilerParams(
            collective_id=collective_id,
            has_side_effects=True,
            vmem_limit_bytes=50 * 1024 * 1024,
        ),
        cost_estimate=pl.CostEstimate(
            flops=2 * count * depth * width * size,
            bytes_accessed=300_000_000,
            transcendentals=0,
        ),
        name="product_scatter",
    )(rows, weight)


def head_weights(cross_key, cross_value):
    fsdp_size, img_size = lax.axis_size("fsdp"), lax.axis_size("img")
    my_shard = lax.axis_index("img")
    rows = cross_key.shape[0]
    part = cross_key.shape[1] // (fsdp_size * img_size)

    def mine(weight):
        split = weight.reshape(rows, fsdp_size, img_size, part)
        return lax.dynamic_index_in_dim(split, my_shard, 2, keepdims=False)

    both = jnp.concatenate([mine(cross_key), mine(cross_value)], 2)
    both = jnp.transpose(both, (1, 0, 2))
    both = lax.all_to_all(both, "fsdp", split_axis=0, concat_axis=0, tiled=True)
    return lax.all_gather(both.reshape(fsdp_size * rows, 2 * part), "img", axis=0)


def local(
    text_states,
    text_gain,
    gate_scale,
    live_counts,
    token_slot,
    wanted_images,
    patches,
    latent_init,
    context_gain,
    latent_gain,
    res_query,
    res_key,
    res_value,
    res_out,
    final_gain,
    cross_query,
    cross_key,
    cross_value,
    cross_out,
):
    my_feature = lax.axis_index("fsdp")
    my_shard = lax.axis_index("img")
    image_count = patches.shape[0]
    patch_count = patches.shape[1]
    feat_vis = patches.shape[2]
    latent_count = latent_init.shape[0]
    vis_width = latent_init.shape[1]
    res_cols = res_query.shape[1]
    res_heads = res_cols // RHD
    head_cols = cross_out.shape[0]
    token_count = text_states.shape[0]
    slot_count = wanted_images.shape[1]
    cross_heads = head_cols // HEAD
    text_f = text_states.astype(jnp.float32)
    full_patches = lax.all_gather(patches, "fsdp", axis=2, tiled=True)
    gain_rows = lax.dynamic_update_slice_in_dim(
        jnp.zeros((vis_width,), jnp.float32), final_gain, my_feature * feat_vis, 0
    )
    shared = lax.psum(jnp.concatenate([jnp.sum(text_f * text_f, -1), gain_rows]), "fsdp")
    squares, full_gain = shared[:token_count], shared[token_count:]
    kv_weights = head_weights(cross_key, cross_value)
    query = product_scatter((text_f * text_gain).astype(jnp.bfloat16), cross_query, 0)
    query = (query * lax.rsqrt(squares / D + eps_rms)[:, None]).astype(jnp.bfloat16)
    context = layer_norm(full_patches, context_gain).astype(jnp.bfloat16)
    latent_normed = layer_norm(latent_init, latent_gain).astype(jnp.bfloat16)
    res_q_rows = jnp.dot(latent_normed, res_query, preferred_element_type=jnp.float32).astype(
        jnp.bfloat16
    )
    res_q_rows = res_q_rows.reshape(latent_count, res_heads, RHD)
    ctx_keys = jnp.einsum(
        "npv,vk->npk", context, res_key, preferred_element_type=jnp.float32
    ).astype(jnp.bfloat16)
    ctx_values = jnp.einsum(
        "npv,vk->npk", context, res_value, preferred_element_type=jnp.float32
    ).astype(jnp.bfloat16)
    lat_keys = jnp.dot(latent_normed, res_key, preferred_element_type=jnp.float32).astype(
        jnp.bfloat16
    )
    lat_values = jnp.dot(latent_normed, res_value, preferred_element_type=jnp.float32).astype(
        jnp.bfloat16
    )
    joined_shape = (image_count, latent_count, res_cols)
    key_rows = jnp.concatenate([ctx_keys, jnp.broadcast_to(lat_keys[None], joined_shape)], 1)
    value_rows = jnp.concatenate([ctx_values, jnp.broadcast_to(lat_values[None], joined_shape)], 1)
    key_rows = key_rows.reshape(image_count, patch_count + latent_count, res_heads, RHD)
    value_rows = value_rows.reshape(image_count, patch_count + latent_count, res_heads, RHD)
    res_scores = jnp.einsum(
        "rhe,nkhe->nhrk", res_q_rows, key_rows, preferred_element_type=jnp.float32
    ) * RHD ** (-0.5)
    res_weights = jnp.exp(res_scores)
    res_weights = (res_weights / jnp.sum(res_weights, -1, keepdims=True)).astype(jnp.bfloat16)
    res_mixed = jnp.einsum(
        "nhrk,nkhe->nrhe", res_weights, value_rows, preferred_element_type=jnp.float32
    )
    res_mixed = res_mixed.astype(jnp.bfloat16).reshape(image_count * latent_count, res_cols)
    mixed_rows = lax.psum_scatter(
        jnp.dot(res_mixed, res_out, preferred_element_type=jnp.float32).astype(jnp.bfloat16),
        "fsdp",
        scatter_dimension=0,
        tiled=True,
    ).astype(jnp.float32)
    row_count = mixed_rows.shape[0]
    init_rows = lax.dynamic_slice_in_dim(
        latent_init, (my_feature * row_count) % latent_count, row_count, 0
    ).astype(jnp.float32)
    resampled = layer_norm(init_rows + mixed_rows, full_gain).astype(jnp.bfloat16)
    resampled = lax.all_gather(resampled, "fsdp", axis=0, tiled=True)
    per_image = resampled.reshape(image_count, latent_count * vis_width)
    outgoing = pack_rows(per_image, wanted_images, my_shard, image_count, PAIR)
    incoming = lax.all_to_all(outgoing, "img", split_axis=0, concat_axis=0, tiled=True)
    slot_latents = unpack_rows(incoming, wanted_images, my_shard, image_count, PAIR).reshape(
        slot_count * latent_count, vis_width
    )
    slot_kv = jnp.einsum(
        "lv,ivk->ilk", slot_latents, kv_weights, preferred_element_type=jnp.float32
    ).astype(jnp.bfloat16)
    slot_kv = slot_kv.reshape(kv_weights.shape[0], slot_count * latent_count, 2, -1)
    slot_kv = jnp.transpose(slot_kv, (2, 0, 3, 1)).reshape(2, cross_heads, HEAD, -1)
    slot_keys, slot_values = slot_kv[0], slot_kv[1]
    query_heads = jnp.transpose(query.reshape(token_count, cross_heads, HEAD), (1, 0, 2))
    scores = jnp.einsum(
        "hte,hel->htl", query_heads, slot_keys, preferred_element_type=jnp.float32
    ) * HEAD ** (-0.5)
    key_slot = jnp.arange(slot_count * latent_count, dtype=jnp.int32) // latent_count
    slot_hot = (token_slot[0][:, None] == key_slot[None, :]).astype(jnp.float32)
    weights = jnp.exp(scores) * slot_hot[None]
    weights = (weights / jnp.sum(weights, axis=2, keepdims=True)).astype(jnp.bfloat16)
    attended = jnp.einsum("htl,hel->the", weights, slot_values, preferred_element_type=jnp.float32)
    attended = attended.astype(jnp.bfloat16).reshape(token_count, head_cols)
    projected = product_scatter(attended, cross_out, 1)
    positions = jnp.arange(token_count, dtype=jnp.int32)
    live_mask = (positions < live_counts[0]).astype(jnp.float32)[:, None]
    return text_f + jnp.tanh(gate_scale) * projected * live_mask


def solution(mesh):
    placed = (
        P("img", "fsdp"),
        P("fsdp"),
        P("fsdp"),
        P("img"),
        P("img", None),
        P(),
        P("img", None, "fsdp"),
        P(),
        P(),
        P(),
        P(None, "fsdp"),
        P(None, "fsdp"),
        P(None, "fsdp"),
        P("fsdp", None),
        P("fsdp"),
        P("fsdp", None),
        P("fsdp", None),
        P("fsdp", None),
        P("fsdp", None),
    )
    return jax.shard_map(
        local, mesh=mesh, in_specs=placed, out_specs=P("img", "fsdp"), check_vma=False
    )
```

```python
import functools

import jax
import jax.numpy as jnp
from jax import lax
from jax.experimental import pallas as pl
from jax.experimental.pallas import tpu as pltpu
from jax.sharding import PartitionSpec as P

D = 8192
HEAD = 128
RHD = 96
PAIR = 2


eps_norm = 1e-05
eps_rms = 1e-06


def layer_norm(values, gain_vec):
    values = values.astype(jnp.float32)
    row_mean = jnp.mean(values, -1, keepdims=True)
    spread = jnp.mean(values * values, -1, keepdims=True) - row_mean * row_mean
    return (values - row_mean) * lax.rsqrt(spread + eps_norm) * gain_vec


def route_tables(wanted_images, per_owner, pair_slots):
    owners = wanted_images // per_owner
    slot_total = wanted_images.shape[1]
    positions = jnp.arange(slot_total, dtype=jnp.int32)
    before = (owners[:, :, None] == owners[:, None, :]) & (
        positions[None, None, :] < positions[None, :, None]
    )
    slot_rank = jnp.sum(before.astype(jnp.int32), axis=2)
    rank_hot = (
        slot_rank[:, :, None] == jnp.arange(pair_slots, dtype=jnp.int32)[None, None, :]
    ).astype(jnp.float32)
    return (owners, rank_hot)


def pack_rows(row_data, wanted_images, my_shard, per_owner, pair_slots):
    owners, rank_hot = route_tables(wanted_images, per_owner, pair_slots)
    is_mine = (owners == my_shard).astype(jnp.float32)
    local_hot = (
        (wanted_images % per_owner)[:, :, None]
        == jnp.arange(per_owner, dtype=jnp.int32)[None, None, :]
    ).astype(jnp.float32)
    picker = jnp.einsum("scp,sci->spi", rank_hot * is_mine[:, :, None], local_hot).astype(
        jnp.bfloat16
    )
    return jnp.einsum("spi,if->spf", picker, row_data, preferred_element_type=jnp.float32).astype(
        jnp.bfloat16
    )


def unpack_rows(received, wanted_images, my_shard, per_owner, pair_slots):
    owners, rank_hot = route_tables(wanted_images, per_owner, pair_slots)
    owner_row = lax.dynamic_slice_in_dim(owners, my_shard, 1, 0)[0]
    rank_row = lax.dynamic_slice_in_dim(rank_hot, my_shard, 1, 0)[0]
    source_hot = (
        owner_row[:, None] == jnp.arange(received.shape[0], dtype=jnp.int32)[None, :]
    ).astype(jnp.float32)
    taker = (source_hot[:, :, None] * rank_row[:, None, :]).astype(jnp.bfloat16)
    return jnp.einsum("cop,opf->cf", taker, received, preferred_element_type=jnp.float32).astype(
        jnp.bfloat16
    )


MESH = pl.DeviceIdType.MESH
LINE = 4
HALVES = 2
TILE = 256
LANES = 128
SPARE_ROWS = 2


def remote(src, dst, send, recv, target):
    return pltpu.make_async_remote_copy(
        src_ref=src,
        dst_ref=dst,
        send_sem=send,
        recv_sem=recv,
        device_id={"fsdp": target},
        device_id_type=MESH,
    )


def product_scatter_kernel(
    rows_ref, weight_ref, out_ref,
    weight, own, x_out, x_in, z_out, z_in,
    w_sem, x_send, x_recv, z_send, z_recv,
):
    me = lax.axis_index("fsdp")
    line, side = me // 2, me % 2
    across = line * 2 + (1 - side)
    is_end = (line == 0) | (line == LINE - 1)
    is_mid = jnp.logical_not(is_end)
    low = line < 2
    near_line = jnp.where(line % 2 == 0, line + 1, line - 1)
    near = near_line * 2 + side
    other_mid = (LINE - 1 - line) * 2 + side
    places = (
        jnp.where(low, 3, 0),
        jnp.where(low, 2, 1),
        near_line,
        line,
    )
    width = weight.shape[2]
    half = width // HALVES

    def fetch(slot):
        step, part = slot % LINE, slot // LINE
        block = places[step] * 2 + (side if part else 1 - side)
        return pltpu.make_async_copy(
            weight_ref.at[:, pl.ds(pl.multiple_of(block * width, width), width)],
            weight.at[slot],
            w_sem.at[slot],
        )

    for slot in range(2 * LINE):
        fetch(slot).start()

    barrier = pltpu.get_barrier_semaphore()
    for target in (across, near):
        pl.semaphore_signal(barrier, inc=1, device_id={"fsdp": target}, device_id_type=MESH)

    @pl.when(is_mid)
    def _():
        pl.semaphore_signal(barrier, inc=1, device_id={"fsdp": other_mid}, device_id_type=MESH)
        pl.semaphore_wait(barrier, 3)

    @pl.when(is_end)
    def _():
        pl.semaphore_wait(barrier, 2)

    def multiply(slot, into, step):
        for h in range(HALVES):

            def tile(c, carry, h=h):
                lower = pl.multiple_of(c * TILE, TILE)
                into[step, h, :, pl.ds(lower, TILE)] = jnp.dot(
                    rows_ref[...],
                    weight[slot, :, pl.ds(pl.multiple_of(h * half + lower, TILE), TILE)],
                    preferred_element_type=jnp.float32,
                ).astype(into.dtype)
                return carry

            lax.fori_loop(0, half // TILE, tile, 0)

    def x_copy(step, h):
        return remote(
            x_out.at[step, h], x_in.at[step, h], x_send.at[step, h], x_recv.at[step, h], across
        )

    def z_copy(step, h):
        if step < 2:
            slot, target = jnp.where(is_end, step, 3 + step), jnp.where(is_end, near, other_mid)
        else:
            slot, target = jnp.where(is_end, 2, 0), near
        return remote(
            z_out.at[step, h], z_in.at[slot, h], z_send.at[step, h], z_recv.at[slot, h], target
        )

    def z_arrived(slot, h):
        remote(
            z_out.at[0, h], z_in.at[slot, h], z_send.at[0, h], z_recv.at[slot, h], near
        ).wait_recv()

    for step in range(LINE):
        fetch(step).wait()
        multiply(step, x_out, step)
        for h in range(HALVES):
            x_copy(step, h).start()
    for step in range(LINE):
        fetch(LINE + step).wait()
        multiply(LINE + step, own, step)

    for step in range(LINE):
        for h in range(HALVES):
            x_copy(step, h).wait_recv()
            if step < LINE - 1:
                arriving = step if step < 2 else 3

                @pl.when(is_end)
                def _(step=step, h=h):
                    z_out[step, h] = (
                        own[step, h].astype(jnp.float32) + x_in[step, h].astype(jnp.float32)
                    ).astype(z_out.dtype)

                @pl.when(is_mid)
                def _(step=step, h=h, arriving=arriving):
                    z_arrived(arriving, h)
                    z_out[step, h] = (
                        own[step, h].astype(jnp.float32)
                        + x_in[step, h].astype(jnp.float32)
                        + z_in[arriving, h].astype(jnp.float32)
                    ).astype(z_out.dtype)

                z_copy(step, h).start()
            else:

                @pl.when(is_end)
                def _(step=step, h=h):
                    z_arrived(0, h)
                    out_ref[:, h * half : (h + 1) * half] = (
                        own[step, h].astype(jnp.float32)
                        + x_in[step, h].astype(jnp.float32)
                        + z_in[0, h].astype(jnp.float32)
                    )

                @pl.when(is_mid)
                def _(step=step, h=h):
                    z_arrived(2, h)
                    z_arrived(4, h)
                    out_ref[:, h * half : (h + 1) * half] = (
                        own[step, h].astype(jnp.float32)
                        + x_in[step, h].astype(jnp.float32)
                        + z_in[2, h].astype(jnp.float32)
                        + z_in[4, h].astype(jnp.float32)
                    )

    for step in range(LINE):
        for h in range(HALVES):
            x_copy(step, h).wait_send()
            if step < LINE - 1:
                z_copy(step, h).wait_send()


def product_scatter(rows, weight, collective_id):
    size = lax.axis_size("fsdp")
    if size != 2 * LINE:
        part = jnp.dot(rows, weight, preferred_element_type=jnp.float32).astype(jnp.bfloat16)
        return lax.psum_scatter(part, "fsdp", scatter_dimension=1, tiled=True).astype(jnp.float32)
    count, depth = rows.shape
    width = weight.shape[1] // size
    unit = (HALVES, count, width // HALVES)
    return pl.pallas_call(
        product_scatter_kernel,
        out_shape=jax.ShapeDtypeStruct((count, width), jnp.float32),
        in_specs=[
            pl.BlockSpec(memory_space=pltpu.VMEM),
            pl.BlockSpec(memory_space=pl.ANY),
        ],
        out_specs=pl.BlockSpec(memory_space=pltpu.VMEM),
        scratch_shapes=[
            pltpu.VMEM((2 * LINE, depth, width), jnp.bfloat16),
            pltpu.VMEM((LINE,) + unit, jnp.bfloat16),
            pltpu.VMEM((LINE,) + unit, jnp.bfloat16),
            pltpu.VMEM((LINE,) + unit, jnp.bfloat16),
            pltpu.VMEM((LINE - 1,) + unit, jnp.bfloat16),
            pltpu.VMEM((LINE + 1,) + unit, jnp.bfloat16),
            pltpu.SemaphoreType.DMA((2 * LINE,)),
            pltpu.SemaphoreType.DMA((LINE, HALVES)),
            pltpu.SemaphoreType.DMA((LINE, HALVES)),
            pltpu.SemaphoreType.DMA((LINE - 1, HALVES)),
            pltpu.SemaphoreType.DMA((LINE + 1, HALVES)),
        ],
        compiler_params=pltpu.CompilerParams(
            collective_id=collective_id,
            has_side_effects=True,
            vmem_limit_bytes=50 * 1024 * 1024,
        ),
        cost_estimate=pl.CostEstimate(
            flops=2 * count * depth * width * size,
            bytes_accessed=300_000_000,
            transcendentals=0,
        ),
        name="product_scatter",
    )(rows, weight)


def latents_kernel(
    part_ref, init_ref, stats_ref, rows_ref, sums_ref,
    part_in, rows_out, rows_in, stats_in,
    part_send, part_recv, rows_send, rows_recv, stats_send, stats_recv,
):
    me = lax.axis_index("fsdp")
    size = part_in.shape[0] + 1
    count = init_ref.shape[0]
    peers = [lax.rem(me + step, size) for step in range(1, size)]
    owners = [lax.rem(me + size - step, size) for step in range(1, size)]

    barrier = pltpu.get_barrier_semaphore()
    for target in peers:
        pl.semaphore_signal(barrier, inc=1, device_id={"fsdp": target}, device_id_type=MESH)
    pl.semaphore_wait(barrier, size - 1)

    def block(owner):
        return pl.ds(pl.multiple_of(owner * count, count), count)

    def stats_copy(i):
        return remote(stats_ref, stats_in.at[i], stats_send.at[i], stats_recv.at[i], peers[i])

    def part_copy(i):
        return remote(
            part_ref.at[block(peers[i]), :], part_in.at[i], part_send.at[i], part_recv.at[i],
            peers[i],
        )

    def rows_copy(i):
        return remote(rows_out, rows_in.at[i], rows_send.at[i], rows_recv.at[i], peers[i])

    for i in range(size - 1):
        part_copy(i).start()
        stats_copy(i).start()
    total = init_ref[...] + part_ref[block(me), :].astype(jnp.float32)
    sums = stats_ref[...]
    for i in range(size - 1):
        part_copy(i).wait_recv()
        stats_copy(i).wait_recv()
        total = total + part_in[i].astype(jnp.float32)
        sums = sums + stats_in[i]
    sums_ref[...] = sums
    first = sums.shape[0] - SPARE_ROWS - total.shape[1] // LANES
    gain = jnp.concatenate(
        [sums[first + r : first + r + 1, :] for r in range(total.shape[1] // LANES)], axis=1
    )
    rows_out[...] = layer_norm(total, gain).astype(rows_out.dtype)
    for i in range(size - 1):
        rows_copy(i).start()
    rows_ref[block(me), :] = rows_out[...]
    for i in range(size - 1):
        rows_copy(i).wait_recv()
        rows_ref[block(owners[i]), :] = rows_in[i]
    for i in range(size - 1):
        part_copy(i).wait_send()
        stats_copy(i).wait_send()
        rows_copy(i).wait_send()


def normed_latents(part, init_rows, stats):
    others = lax.axis_size("fsdp") - 1
    count, width = init_rows.shape
    return pl.pallas_call(
        latents_kernel,
        out_shape=(
            jax.ShapeDtypeStruct(part.shape, jnp.bfloat16),
            jax.ShapeDtypeStruct(stats.shape, jnp.float32),
        ),
        in_specs=[pl.BlockSpec(memory_space=pltpu.VMEM)] * 3,
        out_specs=(pl.BlockSpec(memory_space=pltpu.VMEM),) * 2,
        scratch_shapes=[
            pltpu.VMEM((others, count, width), jnp.bfloat16),
            pltpu.VMEM((count, width), jnp.bfloat16),
            pltpu.VMEM((others, count, width), jnp.bfloat16),
            pltpu.VMEM((others,) + stats.shape, jnp.float32),
        ]
        + [pltpu.SemaphoreType.DMA((others,))] * 6,
        compiler_params=pltpu.CompilerParams(
            collective_id=2, has_side_effects=True, vmem_limit_bytes=16 * 1024 * 1024
        ),
        cost_estimate=pl.CostEstimate(
            flops=part.size * 20, bytes_accessed=100_000_000, transcendentals=0
        ),
        name="normed_latents",
    )(part, init_rows, stats)


def pick_kernel(shard_ref, key_ref, value_ref, out_ref):
    width = key_ref.shape[1]
    out_ref[0, :, :width] = key_ref[...]
    out_ref[0, :, width:] = value_ref[...]


def pick_columns(cross_key, cross_value, parts, stride, part):
    rows = cross_key.shape[0]
    column = pl.BlockSpec((rows, part), lambda b, shard: (0, b * stride + shard[0]))
    return pl.pallas_call(
        pick_kernel,
        out_shape=jax.ShapeDtypeStruct((parts, rows, 2 * part), cross_key.dtype),
        grid_spec=pltpu.PrefetchScalarGridSpec(
            num_scalar_prefetch=1,
            grid=(parts,),
            in_specs=[column, column],
            out_specs=pl.BlockSpec((1, rows, 2 * part), lambda b, shard: (b, 0, 0)),
        ),
        name="pick_columns",
    )(lax.axis_index("img").astype(jnp.int32).reshape(1), cross_key, cross_value)


def head_weights(cross_key, cross_value):
    fsdp_size, img_size = lax.axis_size("fsdp"), lax.axis_size("img")
    my_shard = lax.axis_index("img")
    rows = cross_key.shape[0]
    part = cross_key.shape[1] // (fsdp_size * img_size)

    def mine(weight):
        split = weight.reshape(rows, fsdp_size, img_size, part)
        return lax.dynamic_index_in_dim(split, my_shard, 2, keepdims=False)

    if part % LANES == 0:
        both = pick_columns(cross_key, cross_value, fsdp_size, img_size, part)
    else:
        both = jnp.concatenate([mine(cross_key), mine(cross_value)], 2)
        both = jnp.transpose(both, (1, 0, 2))
    both = lax.all_to_all(both, "fsdp", split_axis=0, concat_axis=0, tiled=True)
    return lax.all_gather(both.reshape(fsdp_size * rows, 2 * part), "img", axis=0)


def local(
    text_states,
    text_gain,
    gate_scale,
    live_counts,
    token_slot,
    wanted_images,
    patches,
    latent_init,
    context_gain,
    latent_gain,
    res_query,
    res_key,
    res_value,
    res_out,
    final_gain,
    cross_query,
    cross_key,
    cross_value,
    cross_out,
):
    my_feature = lax.axis_index("fsdp")
    my_shard = lax.axis_index("img")
    image_count = patches.shape[0]
    patch_count = patches.shape[1]
    feat_vis = patches.shape[2]
    latent_count = latent_init.shape[0]
    vis_width = latent_init.shape[1]
    res_cols = res_query.shape[1]
    res_heads = res_cols // RHD
    head_cols = cross_out.shape[0]
    token_count = text_states.shape[0]
    slot_count = wanted_images.shape[1]
    cross_heads = head_cols // HEAD
    text_f = text_states.astype(jnp.float32)
    full_patches = lax.all_gather(patches, "fsdp", axis=2, tiled=True)
    gain_rows = lax.dynamic_update_slice_in_dim(
        jnp.zeros((vis_width,), jnp.float32), final_gain, my_feature * feat_vis, 0
    )
    stats = jnp.concatenate(
        [jnp.sum(text_f * text_f, -1), gain_rows, jnp.zeros((SPARE_ROWS * LANES,), jnp.float32)]
    ).reshape(-1, LANES)
    kv_weights = head_weights(cross_key, cross_value)
    query = product_scatter((text_f * text_gain).astype(jnp.bfloat16), cross_query, 0)
    full_patches, query = lax.optimization_barrier((full_patches, query))
    context = layer_norm(full_patches, context_gain).astype(jnp.bfloat16)
    latent_normed = layer_norm(latent_init, latent_gain).astype(jnp.bfloat16)
    res_q_rows = jnp.dot(latent_normed, res_query, preferred_element_type=jnp.float32).astype(
        jnp.bfloat16
    )
    res_q_rows = res_q_rows.reshape(latent_count, res_heads, RHD)
    ctx_keys = jnp.einsum(
        "npv,vk->npk", context, res_key, preferred_element_type=jnp.float32
    ).astype(jnp.bfloat16)
    ctx_values = jnp.einsum(
        "npv,vk->npk", context, res_value, preferred_element_type=jnp.float32
    ).astype(jnp.bfloat16)
    lat_keys = jnp.dot(latent_normed, res_key, preferred_element_type=jnp.float32).astype(
        jnp.bfloat16
    )
    lat_values = jnp.dot(latent_normed, res_value, preferred_element_type=jnp.float32).astype(
        jnp.bfloat16
    )
    joined_shape = (image_count, latent_count, res_cols)
    key_rows = jnp.concatenate([ctx_keys, jnp.broadcast_to(lat_keys[None], joined_shape)], 1)
    value_rows = jnp.concatenate([ctx_values, jnp.broadcast_to(lat_values[None], joined_shape)], 1)
    key_rows = key_rows.reshape(image_count, patch_count + latent_count, res_heads, RHD)
    value_rows = value_rows.reshape(image_count, patch_count + latent_count, res_heads, RHD)
    res_scores = jnp.einsum(
        "rhe,nkhe->nhrk", res_q_rows, key_rows, preferred_element_type=jnp.float32
    ) * RHD ** (-0.5)
    res_weights = jnp.exp(res_scores)
    res_weights = (res_weights / jnp.sum(res_weights, -1, keepdims=True)).astype(jnp.bfloat16)
    res_mixed = jnp.einsum(
        "nhrk,nkhe->nrhe", res_weights, value_rows, preferred_element_type=jnp.float32
    )
    res_mixed = res_mixed.astype(jnp.bfloat16).reshape(image_count * latent_count, res_cols)
    mixed_part = jnp.dot(res_mixed, res_out, preferred_element_type=jnp.float32)
    row_count = mixed_part.shape[0] // lax.axis_size("fsdp")
    init_rows = lax.dynamic_slice_in_dim(
        latent_init, (my_feature * row_count) % latent_count, row_count, 0
    ).astype(jnp.float32)
    resampled, sums = normed_latents(mixed_part.astype(jnp.bfloat16), init_rows, stats)
    squares = sums.reshape(-1)[:token_count]
    query = (query * lax.rsqrt(squares / D + eps_rms)[:, None]).astype(jnp.bfloat16)
    per_image = resampled.reshape(image_count, latent_count * vis_width)
    outgoing = pack_rows(per_image, wanted_images, my_shard, image_count, PAIR)
    incoming = lax.all_to_all(outgoing, "img", split_axis=0, concat_axis=0, tiled=True)
    slot_latents = unpack_rows(incoming, wanted_images, my_shard, image_count, PAIR).reshape(
        slot_count * latent_count, vis_width
    )
    slot_kv = jnp.einsum(
        "lv,ivk->ilk", slot_latents, kv_weights, preferred_element_type=jnp.float32
    ).astype(jnp.bfloat16)
    slot_kv = slot_kv.reshape(kv_weights.shape[0], slot_count * latent_count, 2, -1)
    slot_kv = jnp.transpose(slot_kv, (2, 0, 3, 1)).reshape(2, cross_heads, HEAD, -1)
    slot_keys, slot_values = slot_kv[0], slot_kv[1]
    query_heads = jnp.transpose(query.reshape(token_count, cross_heads, HEAD), (1, 0, 2))
    scores = jnp.einsum(
        "hte,hel->htl", query_heads, slot_keys, preferred_element_type=jnp.float32
    ) * HEAD ** (-0.5)
    key_slot = jnp.arange(slot_count * latent_count, dtype=jnp.int32) // latent_count
    slot_hot = (token_slot[0][:, None] == key_slot[None, :]).astype(jnp.float32)
    weights = jnp.exp(scores) * slot_hot[None]
    weights = (weights / jnp.sum(weights, axis=2, keepdims=True)).astype(jnp.bfloat16)
    attended = jnp.einsum("htl,hel->the", weights, slot_values, preferred_element_type=jnp.float32)
    attended = attended.astype(jnp.bfloat16).reshape(token_count, head_cols)
    projected = product_scatter(attended, cross_out, 1)
    positions = jnp.arange(token_count, dtype=jnp.int32)
    live_mask = (positions < live_counts[0]).astype(jnp.float32)[:, None]
    return text_f + jnp.tanh(gate_scale) * projected * live_mask


def solution(mesh):
    placed = (
        P("img", "fsdp"),
        P("fsdp"),
        P("fsdp"),
        P("img"),
        P("img", None),
        P(),
        P("img", None, "fsdp"),
        P(),
        P(),
        P(),
        P(None, "fsdp"),
        P(None, "fsdp"),
        P(None, "fsdp"),
        P("fsdp", None),
        P("fsdp"),
        P("fsdp", None),
        P("fsdp", None),
        P("fsdp", None),
        P("fsdp", None),
    )
    return jax.shard_map(
        local, mesh=mesh, in_specs=placed, out_specs=P("img", "fsdp"), check_vma=False
    )
```

```python
import functools

import jax
import jax.numpy as jnp
from jax import lax
from jax.experimental import pallas as pl
from jax.experimental.pallas import tpu as pltpu
from jax.sharding import PartitionSpec as P

D = 8192
HEAD = 128
RHD = 96
PAIR = 2


eps_norm = 1e-05
eps_rms = 1e-06


def layer_norm(values, gain_vec):
    values = values.astype(jnp.float32)
    row_mean = jnp.mean(values, -1, keepdims=True)
    spread = jnp.mean(values * values, -1, keepdims=True) - row_mean * row_mean
    return (values - row_mean) * lax.rsqrt(spread + eps_norm) * gain_vec


def route_tables(wanted_images, per_owner, pair_slots):
    owners = wanted_images // per_owner
    slot_total = wanted_images.shape[1]
    positions = jnp.arange(slot_total, dtype=jnp.int32)
    before = (owners[:, :, None] == owners[:, None, :]) & (
        positions[None, None, :] < positions[None, :, None]
    )
    slot_rank = jnp.sum(before.astype(jnp.int32), axis=2)
    rank_hot = (
        slot_rank[:, :, None] == jnp.arange(pair_slots, dtype=jnp.int32)[None, None, :]
    ).astype(jnp.float32)
    return (owners, rank_hot)


def pack_rows(row_data, wanted_images, my_shard, per_owner, pair_slots):
    owners, rank_hot = route_tables(wanted_images, per_owner, pair_slots)
    is_mine = (owners == my_shard).astype(jnp.float32)
    local_hot = (
        (wanted_images % per_owner)[:, :, None]
        == jnp.arange(per_owner, dtype=jnp.int32)[None, None, :]
    ).astype(jnp.float32)
    picker = jnp.einsum("scp,sci->spi", rank_hot * is_mine[:, :, None], local_hot).astype(
        jnp.bfloat16
    )
    picked = picker[:, :, 0, None, None] * row_data[0]
    for image in range(1, per_owner):
        picked = picked + picker[:, :, image, None, None] * row_data[image]
    return picked


def arrived_slots(wanted_images, my_shard, per_owner, pair_slots):
    owners, rank_hot = route_tables(wanted_images, per_owner, pair_slots)
    owner_row = lax.dynamic_slice_in_dim(owners, my_shard, 1, 0)[0]
    rank_row = lax.dynamic_slice_in_dim(rank_hot, my_shard, 1, 0)[0].astype(jnp.int32)
    shards, slot_total = wanted_images.shape
    source_hot = (
        owner_row[:, None] == jnp.arange(shards, dtype=jnp.int32)[None, :]
    ).astype(jnp.int32)
    numbered = jnp.arange(1, slot_total + 1, dtype=jnp.int32)[:, None, None]
    return jnp.sum(source_hot[:, :, None] * rank_row[:, None, :] * numbered, 0) - 1


MESH = pl.DeviceIdType.MESH
LINE = 4
HALVES = 2
TILE = 256
LANES = 128
SPARE_ROWS = 2


def remote(src, dst, send, recv, target):
    return pltpu.make_async_remote_copy(
        src_ref=src,
        dst_ref=dst,
        send_sem=send,
        recv_sem=recv,
        device_id={"fsdp": target},
        device_id_type=MESH,
    )


def product_scatter_kernel(exchange, *refs):
    if exchange:
        rows_ref, weight_ref, moved_ref, out_ref, moved_out, *refs = refs
        *refs, moved_in, moved_send, moved_recv = refs
    else:
        rows_ref, weight_ref, out_ref, *refs = refs
    weight, own, x_out, x_in, z_out, z_in, w_sem, x_send, x_recv, z_send, z_recv = refs
    me = lax.axis_index("fsdp")
    size = 2 * LINE
    line, side = me // 2, me % 2
    across = line * 2 + (1 - side)
    is_end = (line == 0) | (line == LINE - 1)
    is_mid = jnp.logical_not(is_end)
    low = line < 2
    near_line = jnp.where(line % 2 == 0, line + 1, line - 1)
    near = near_line * 2 + side
    other_mid = (LINE - 1 - line) * 2 + side
    places = (
        jnp.where(low, 3, 0),
        jnp.where(low, 2, 1),
        near_line,
        line,
    )
    width = weight.shape[2]
    half = width // HALVES

    def fetch(slot):
        step, part = slot % LINE, slot // LINE
        block = places[step] * 2 + (side if part else 1 - side)
        return pltpu.make_async_copy(
            weight_ref.at[:, pl.ds(pl.multiple_of(block * width, width), width)],
            weight.at[slot],
            w_sem.at[slot],
        )

    for slot in range(2 * LINE):
        fetch(slot).start()

    barrier = pltpu.get_barrier_semaphore()
    if exchange:
        for step in range(1, size):
            pl.semaphore_signal(
                barrier, inc=1, device_id={"fsdp": (me + step) % size}, device_id_type=MESH
            )
        pl.semaphore_wait(barrier, size - 1)
    else:
        for target in (across, near):
            pl.semaphore_signal(barrier, inc=1, device_id={"fsdp": target}, device_id_type=MESH)

        @pl.when(is_mid)
        def _():
            pl.semaphore_signal(barrier, inc=1, device_id={"fsdp": other_mid}, device_id_type=MESH)
            pl.semaphore_wait(barrier, 3)

        @pl.when(is_end)
        def _():
            pl.semaphore_wait(barrier, 2)

    def moved_copy(i):
        target = (me + i + 1) % size
        return remote(
            moved_ref.at[target], moved_in.at[i], moved_send.at[i], moved_recv.at[i], target
        )

    def multiply(slot, into, step):
        for h in range(HALVES):

            def tile(c, carry, h=h):
                lower = pl.multiple_of(c * TILE, TILE)
                into[step, h, :, pl.ds(lower, TILE)] = jnp.dot(
                    rows_ref[...],
                    weight[slot, :, pl.ds(pl.multiple_of(h * half + lower, TILE), TILE)],
                    preferred_element_type=jnp.float32,
                ).astype(into.dtype)
                return carry

            lax.fori_loop(0, half // TILE, tile, 0)

    def x_copy(step, h):
        return remote(
            x_out.at[step, h], x_in.at[step, h], x_send.at[step, h], x_recv.at[step, h], across
        )

    def z_copy(step, h):
        if step < 2:
            slot, target = jnp.where(is_end, step, 3 + step), jnp.where(is_end, near, other_mid)
        else:
            slot, target = jnp.where(is_end, 2, 0), near
        return remote(
            z_out.at[step, h], z_in.at[slot, h], z_send.at[step, h], z_recv.at[slot, h], target
        )

    def z_arrived(slot, h):
        remote(
            z_out.at[0, h], z_in.at[slot, h], z_send.at[0, h], z_recv.at[slot, h], near
        ).wait_recv()

    for step in range(LINE):
        fetch(step).wait()
        multiply(step, x_out, step)
        for h in range(HALVES):
            x_copy(step, h).start()
    if exchange:
        for i in range(size - 1):
            moved_copy(i).start()
    for step in range(LINE):
        fetch(LINE + step).wait()
        multiply(LINE + step, own, step)

    for step in range(LINE):
        for h in range(HALVES):
            x_copy(step, h).wait_recv()
            if step < LINE - 1:
                arriving = step if step < 2 else 3

                @pl.when(is_end)
                def _(step=step, h=h):
                    z_out[step, h] = (
                        own[step, h].astype(jnp.float32) + x_in[step, h].astype(jnp.float32)
                    ).astype(z_out.dtype)

                @pl.when(is_mid)
                def _(step=step, h=h, arriving=arriving):
                    z_arrived(arriving, h)
                    z_out[step, h] = (
                        own[step, h].astype(jnp.float32)
                        + x_in[step, h].astype(jnp.float32)
                        + z_in[arriving, h].astype(jnp.float32)
                    ).astype(z_out.dtype)

                z_copy(step, h).start()
            else:

                @pl.when(is_end)
                def _(step=step, h=h):
                    z_arrived(0, h)
                    out_ref[:, h * half : (h + 1) * half] = (
                        own[step, h].astype(jnp.float32)
                        + x_in[step, h].astype(jnp.float32)
                        + z_in[0, h].astype(jnp.float32)
                    )

                @pl.when(is_mid)
                def _(step=step, h=h):
                    z_arrived(2, h)
                    z_arrived(4, h)
                    out_ref[:, h * half : (h + 1) * half] = (
                        own[step, h].astype(jnp.float32)
                        + x_in[step, h].astype(jnp.float32)
                        + z_in[2, h].astype(jnp.float32)
                        + z_in[4, h].astype(jnp.float32)
                    )

    if exchange:
        moved_out[me] = moved_ref[me]
        for i in range(size - 1):
            moved_copy(i).wait_recv()
            moved_out[(me + size - i - 1) % size] = moved_in[i]
            moved_copy(i).wait_send()
    for step in range(LINE):
        for h in range(HALVES):
            x_copy(step, h).wait_send()
            if step < LINE - 1:
                z_copy(step, h).wait_send()


def product_scatter(rows, weight, collective_id, moved=None):
    size = lax.axis_size("fsdp")
    exchange = moved is not None
    if size != 2 * LINE:
        part = jnp.dot(rows, weight, preferred_element_type=jnp.float32).astype(jnp.bfloat16)
        kept = lax.psum_scatter(part, "fsdp", scatter_dimension=1, tiled=True).astype(jnp.float32)
        if not exchange:
            return kept
        return kept, lax.all_to_all(moved, "fsdp", split_axis=0, concat_axis=0, tiled=True)
    count, depth = rows.shape
    width = weight.shape[1] // size
    unit = (HALVES, count, width // HALVES)
    vmem = pl.BlockSpec(memory_space=pltpu.VMEM)
    operands, in_specs = [rows, weight], [vmem, pl.BlockSpec(memory_space=pl.ANY)]
    out_shape, out_specs = [jax.ShapeDtypeStruct((count, width), jnp.float32)], [vmem]
    scratch = [
        pltpu.VMEM((size, depth, width), jnp.bfloat16),
        pltpu.VMEM((LINE,) + unit, jnp.bfloat16),
        pltpu.VMEM((LINE,) + unit, jnp.bfloat16),
        pltpu.VMEM((LINE,) + unit, jnp.bfloat16),
        pltpu.VMEM((LINE - 1,) + unit, jnp.bfloat16),
        pltpu.VMEM((LINE + 1,) + unit, jnp.bfloat16),
        pltpu.SemaphoreType.DMA((size,)),
        pltpu.SemaphoreType.DMA((LINE, HALVES)),
        pltpu.SemaphoreType.DMA((LINE, HALVES)),
        pltpu.SemaphoreType.DMA((LINE - 1, HALVES)),
        pltpu.SemaphoreType.DMA((LINE + 1, HALVES)),
    ]
    if exchange:
        operands.append(moved)
        in_specs.append(vmem)
        out_shape.append(jax.ShapeDtypeStruct(moved.shape, moved.dtype))
        out_specs.append(vmem)
        scratch += [
            pltpu.VMEM((size - 1,) + moved.shape[1:], moved.dtype),
            pltpu.SemaphoreType.DMA((size - 1,)),
            pltpu.SemaphoreType.DMA((size - 1,)),
        ]
    results = pl.pallas_call(
        functools.partial(product_scatter_kernel, exchange),
        out_shape=out_shape,
        in_specs=in_specs,
        out_specs=out_specs,
        scratch_shapes=scratch,
        compiler_params=pltpu.CompilerParams(
            collective_id=collective_id,
            has_side_effects=True,
            vmem_limit_bytes=52 * 1024 * 1024,
        ),
        cost_estimate=pl.CostEstimate(
            flops=2 * count * depth * width * size,
            bytes_accessed=300_000_000,
            transcendentals=0,
        ),
        name="product_scatter",
    )(*operands)
    return results if exchange else results[0]


def latents_kernel(
    part_ref, init_ref, stats_ref, rows_ref, sums_ref,
    part_in, rows_out, rows_in, stats_in,
    part_send, part_recv, rows_send, rows_recv, stats_send, stats_recv,
):
    me = lax.axis_index("fsdp")
    size = part_in.shape[0] + 1
    count = init_ref.shape[0]
    peers = [lax.rem(me + step, size) for step in range(1, size)]
    owners = [lax.rem(me + size - step, size) for step in range(1, size)]

    barrier = pltpu.get_barrier_semaphore()
    for target in peers:
        pl.semaphore_signal(barrier, inc=1, device_id={"fsdp": target}, device_id_type=MESH)
    pl.semaphore_wait(barrier, size - 1)

    def block(owner):
        return pl.ds(pl.multiple_of(owner * count, count), count)

    def stats_copy(i):
        return remote(stats_ref, stats_in.at[i], stats_send.at[i], stats_recv.at[i], peers[i])

    def part_copy(i):
        return remote(
            part_ref.at[block(peers[i]), :], part_in.at[i], part_send.at[i], part_recv.at[i],
            peers[i],
        )

    def rows_copy(i):
        return remote(rows_out, rows_in.at[i], rows_send.at[i], rows_recv.at[i], peers[i])

    for i in range(size - 1):
        part_copy(i).start()
        stats_copy(i).start()
    total = init_ref[...] + part_ref[block(me), :].astype(jnp.float32)
    sums = stats_ref[...]
    for i in range(size - 1):
        part_copy(i).wait_recv()
        stats_copy(i).wait_recv()
        total = total + part_in[i].astype(jnp.float32)
        sums = sums + stats_in[i]
    sums_ref[...] = sums
    first = sums.shape[0] - SPARE_ROWS - total.shape[1] // LANES
    gain = jnp.concatenate(
        [sums[first + r : first + r + 1, :] for r in range(total.shape[1] // LANES)], axis=1
    )
    rows_out[...] = layer_norm(total, gain).astype(rows_out.dtype)
    for i in range(size - 1):
        rows_copy(i).start()
    rows_ref[block(me), :] = rows_out[...]
    for i in range(size - 1):
        rows_copy(i).wait_recv()
        rows_ref[block(owners[i]), :] = rows_in[i]
    for i in range(size - 1):
        part_copy(i).wait_send()
        stats_copy(i).wait_send()
        rows_copy(i).wait_send()


def normed_latents(part, init_rows, stats):
    others = lax.axis_size("fsdp") - 1
    count, width = init_rows.shape
    return pl.pallas_call(
        latents_kernel,
        out_shape=(
            jax.ShapeDtypeStruct(part.shape, jnp.bfloat16),
            jax.ShapeDtypeStruct(stats.shape, jnp.float32),
        ),
        in_specs=[pl.BlockSpec(memory_space=pltpu.VMEM)] * 3,
        out_specs=(pl.BlockSpec(memory_space=pltpu.VMEM),) * 2,
        scratch_shapes=[
            pltpu.VMEM((others, count, width), jnp.bfloat16),
            pltpu.VMEM((count, width), jnp.bfloat16),
            pltpu.VMEM((others, count, width), jnp.bfloat16),
            pltpu.VMEM((others,) + stats.shape, jnp.float32),
        ]
        + [pltpu.SemaphoreType.DMA((others,))] * 6,
        compiler_params=pltpu.CompilerParams(
            collective_id=2, has_side_effects=True, vmem_limit_bytes=16 * 1024 * 1024
        ),
        cost_estimate=pl.CostEstimate(
            flops=part.size * 20, bytes_accessed=100_000_000, transcendentals=0
        ),
        name="normed_latents",
    )(part, init_rows, stats)


def pick_kernel(shard_ref, key_ref, value_ref, out_ref):
    width = key_ref.shape[1]
    out_ref[0, :, :width] = key_ref[...]
    out_ref[0, :, width:] = value_ref[...]


def pick_columns(cross_key, cross_value, parts, stride, part):
    rows = cross_key.shape[0]
    column = pl.BlockSpec((rows, part), lambda b, shard: (0, b * stride + shard[0]))
    return pl.pallas_call(
        pick_kernel,
        out_shape=jax.ShapeDtypeStruct((parts, rows, 2 * part), cross_key.dtype),
        grid_spec=pltpu.PrefetchScalarGridSpec(
            num_scalar_prefetch=1,
            grid=(parts,),
            in_specs=[column, column],
            out_specs=pl.BlockSpec((1, rows, 2 * part), lambda b, shard: (b, 0, 0)),
        ),
        name="pick_columns",
    )(lax.axis_index("img").astype(jnp.int32).reshape(1), cross_key, cross_value)


def weight_blocks(cross_key, cross_value):
    fsdp_size, img_size = lax.axis_size("fsdp"), lax.axis_size("img")
    my_shard = lax.axis_index("img")
    rows = cross_key.shape[0]
    part = cross_key.shape[1] // (fsdp_size * img_size)

    def mine(weight):
        split = weight.reshape(rows, fsdp_size, img_size, part)
        return lax.dynamic_index_in_dim(split, my_shard, 2, keepdims=False)

    if part % LANES == 0:
        return pick_columns(cross_key, cross_value, fsdp_size, img_size, part)
    both = jnp.concatenate([mine(cross_key), mine(cross_value)], 2)
    return jnp.transpose(both, (1, 0, 2))


def local(
    text_states,
    text_gain,
    gate_scale,
    live_counts,
    token_slot,
    wanted_images,
    patches,
    latent_init,
    context_gain,
    latent_gain,
    res_query,
    res_key,
    res_value,
    res_out,
    final_gain,
    cross_query,
    cross_key,
    cross_value,
    cross_out,
):
    my_feature = lax.axis_index("fsdp")
    my_shard = lax.axis_index("img")
    image_count = patches.shape[0]
    patch_count = patches.shape[1]
    feat_vis = patches.shape[2]
    latent_count = latent_init.shape[0]
    vis_width = latent_init.shape[1]
    res_cols = res_query.shape[1]
    res_heads = res_cols // RHD
    head_cols = cross_out.shape[0]
    token_count = text_states.shape[0]
    cross_heads = head_cols // HEAD
    text_f = text_states.astype(jnp.float32)
    full_patches = lax.all_gather(patches, "fsdp", axis=2, tiled=True)
    gain_rows = lax.dynamic_update_slice_in_dim(
        jnp.zeros((vis_width,), jnp.float32), final_gain, my_feature * feat_vis, 0
    )
    stats = jnp.concatenate(
        [jnp.sum(text_f * text_f, -1), gain_rows, jnp.zeros((SPARE_ROWS * LANES,), jnp.float32)]
    ).reshape(-1, LANES)
    query, kv_weights = product_scatter(
        (text_f * text_gain).astype(jnp.bfloat16),
        cross_query,
        0,
        weight_blocks(cross_key, cross_value),
    )
    kv_weights = lax.all_gather(kv_weights.reshape(vis_width, -1), "img", axis=0)
    full_patches, query = lax.optimization_barrier((full_patches, query))
    context = layer_norm(full_patches, context_gain).astype(jnp.bfloat16)
    latent_normed = layer_norm(latent_init, latent_gain).astype(jnp.bfloat16)
    res_q_rows = jnp.dot(latent_normed, res_query, preferred_element_type=jnp.float32).astype(
        jnp.bfloat16
    )
    res_q_rows = res_q_rows.reshape(latent_count, res_heads, RHD)
    ctx_keys = jnp.einsum(
        "npv,vk->npk", context, res_key, preferred_element_type=jnp.float32
    ).astype(jnp.bfloat16)
    ctx_values = jnp.einsum(
        "npv,vk->npk", context, res_value, preferred_element_type=jnp.float32
    ).astype(jnp.bfloat16)
    lat_keys = jnp.dot(latent_normed, res_key, preferred_element_type=jnp.float32).astype(
        jnp.bfloat16
    )
    lat_values = jnp.dot(latent_normed, res_value, preferred_element_type=jnp.float32).astype(
        jnp.bfloat16
    )
    joined_shape = (image_count, latent_count, res_cols)
    key_rows = jnp.concatenate([ctx_keys, jnp.broadcast_to(lat_keys[None], joined_shape)], 1)
    value_rows = jnp.concatenate([ctx_values, jnp.broadcast_to(lat_values[None], joined_shape)], 1)
    key_rows = key_rows.reshape(image_count, patch_count + latent_count, res_heads, RHD)
    value_rows = value_rows.reshape(image_count, patch_count + latent_count, res_heads, RHD)
    res_scores = jnp.einsum(
        "rhe,nkhe->nhrk", res_q_rows, key_rows, preferred_element_type=jnp.float32
    ) * RHD ** (-0.5)
    res_weights = jnp.exp(res_scores)
    res_weights = (res_weights / jnp.sum(res_weights, -1, keepdims=True)).astype(jnp.bfloat16)
    res_mixed = jnp.einsum(
        "nhrk,nkhe->nrhe", res_weights, value_rows, preferred_element_type=jnp.float32
    )
    res_mixed = res_mixed.astype(jnp.bfloat16).reshape(image_count * latent_count, res_cols)
    mixed_part = jnp.dot(res_mixed, res_out, preferred_element_type=jnp.float32)
    row_count = mixed_part.shape[0] // lax.axis_size("fsdp")
    init_rows = lax.dynamic_slice_in_dim(
        latent_init, (my_feature * row_count) % latent_count, row_count, 0
    ).astype(jnp.float32)
    resampled, sums = normed_latents(mixed_part.astype(jnp.bfloat16), init_rows, stats)
    squares = sums.reshape(-1)[:token_count]
    query = (query * lax.rsqrt(squares / D + eps_rms)[:, None]).astype(jnp.bfloat16)
    per_image = resampled.reshape(image_count, latent_count, vis_width)
    outgoing = pack_rows(per_image, wanted_images, my_shard, image_count, PAIR)
    outgoing = outgoing.reshape(-1, PAIR * latent_count, vis_width)
    incoming = lax.all_to_all(outgoing, "img", split_axis=0, concat_axis=0, tiled=True)
    slot_latents = incoming.reshape(-1, vis_width)
    arrived = arrived_slots(wanted_images, my_shard, image_count, PAIR)
    slot_kv = jnp.einsum(
        "lv,ivk->ilk", slot_latents, kv_weights, preferred_element_type=jnp.float32
    ).astype(jnp.bfloat16)
    slot_kv = slot_kv.reshape(kv_weights.shape[0], slot_latents.shape[0], 2, -1)
    slot_kv = jnp.transpose(slot_kv, (2, 0, 3, 1)).reshape(2, cross_heads, HEAD, -1)
    slot_keys, slot_values = slot_kv[0], slot_kv[1]
    query_heads = jnp.transpose(query.reshape(token_count, cross_heads, HEAD), (1, 0, 2))
    scores = jnp.einsum(
        "hte,hel->htl", query_heads, slot_keys, preferred_element_type=jnp.float32
    ) * HEAD ** (-0.5)
    key_slot = jnp.repeat(arrived.reshape(-1), latent_count)
    slot_hot = (token_slot[0][:, None] == key_slot[None, :]).astype(jnp.float32)
    weights = jnp.exp(scores) * slot_hot[None]
    weights = (weights / jnp.sum(weights, axis=2, keepdims=True)).astype(jnp.bfloat16)
    attended = jnp.einsum("htl,hel->the", weights, slot_values, preferred_element_type=jnp.float32)
    attended = attended.astype(jnp.bfloat16).reshape(token_count, head_cols)
    projected = product_scatter(attended, cross_out, 1)
    positions = jnp.arange(token_count, dtype=jnp.int32)
    live_mask = (positions < live_counts[0]).astype(jnp.float32)[:, None]
    return text_f + jnp.tanh(gate_scale) * projected * live_mask


def solution(mesh):
    placed = (
        P("img", "fsdp"),
        P("fsdp"),
        P("fsdp"),
        P("img"),
        P("img", None),
        P(),
        P("img", None, "fsdp"),
        P(),
        P(),
        P(),
        P(None, "fsdp"),
        P(None, "fsdp"),
        P(None, "fsdp"),
        P("fsdp", None),
        P("fsdp"),
        P("fsdp", None),
        P("fsdp", None),
        P("fsdp", None),
        P("fsdp", None),
    )
    return jax.shard_map(
        local, mesh=mesh, in_specs=placed, out_specs=P("img", "fsdp"), check_vma=False
    )
```
